256 devices in a mesh: space: 16 (over y, z_lo), vel: 16 (over x, z_hi, core).
Axes of the slice: x: 4, y: 4, z: 8 (z_hi: 2, z_lo: 4; z = z_hi * 4 + z_lo), core: 2. Of those that a mesh axis runs over, the one named last changes fastest.
Arguments:
- distribution: float32 [13824, 64, 128], P('vel', 'space'), as said below
- wall_mask: int32 [64, 128], P('space'), may hold values from 0 to 1, as said below
Outputs:
- evolved: float32 [13824, 64, 128], P('vel', 'space')
The draws below stay inside these ranges and needn't reach their ends.
Inputs may be any that keep to these rules, and one draw needn't show every extreme that they name: `wall_mask`: the cells with 1 are those of two neighbouring x layers p and p + 1 (p + 1 taken modulo 64) over one run of y cells, for one p. `distribution`: every entry is nonnegative.
All inputs are finite; a program needn't handle non-finite values.
Results may differ from the reference program's by a relative error of at most 0.0003.
Values sent between devices are 32-bit elements; how exact they have to be, the bound alone decides.
A program may use at most 64 MiB of HBM per device.

```python
import math
import jax
import jax.numpy as jnp
from jax import lax

NODES = 24
VEL = 13824
VB = 864
NY = 128
STEPS = 2
NX = 64
N_VEL = 16


def node_values(nodes):
    total = nodes ** 3
    plane = nodes * nodes
    index = jnp.arange(total, dtype=jnp.int32)
    upper = index >= total // 2
    folded = jnp.where(upper, total - 1 - index, index)
    xcell = jnp.where(upper, nodes - 1 - folded // plane, folded // plane)
    rest = folded % plane
    spacing = 9.0 / nodes
    return tuple(((cell.astype(jnp.float32) + 0.5) * spacing - 4.5 for cell in (xcell, rest // nodes, rest % nodes)))


def draw_distribution(key, part):
    key = jax.random.fold_in(key, 11)
    keys = jax.random.split(key, 7)
    low, high, flow, rough = (0.05, 2.0, 0.3, 0.3)
    density = jnp.exp(jax.random.uniform(keys[0], (1, NX, NY), jnp.float32, jnp.log(low), jnp.log(high)))
    temper = jnp.exp(jax.random.uniform(keys[1], (1, NX, NY), jnp.float32, jnp.log(0.4), jnp.log(2.0)))
    band_start = jax.random.randint(keys[5], (), 0, NY)
    ycell = jnp.arange(NY, dtype=jnp.int32)[None, None, :]
    in_band = (ycell - band_start) % NY < max(NY // 8, 1)
    cold = jnp.exp(jax.random.uniform(keys[6], (1, NX, NY), jnp.float32, jnp.log(0.02), jnp.log(0.06)))
    temper = jnp.where(in_band, cold, temper)
    density = jnp.where(in_band, density * (temper / 0.4) ** 1.5, density)
    ux = jax.random.uniform(keys[2], (1, NX, NY), jnp.float32, -flow, flow)
    uy = jax.random.uniform(keys[3], (1, NX, NY), jnp.float32, -flow, flow)
    vx, vy, vz = node_values(NODES)
    cx = vx[:, None, None] - ux
    cy = vy[:, None, None] - uy
    cz = vz[:, None, None]
    square = cx * cx + cy * cy + cz * cz
    noise = 1.0 + rough * jax.random.uniform(keys[4], (VEL, NX, NY), jnp.float32, -1.0, 1.0)
    return (density * temper ** (-1.5) * jnp.exp(-square / (2.0 * temper)) * noise).astype(jnp.float32)


def draw_wall_mask(key, part):
    key = jax.random.fold_in(key, 23)
    keys = jax.random.split(key, 3)
    layer = jax.random.randint(keys[0], (), 0, NX)
    span = jax.random.randint(keys[1], (), NY // 4, 3 * NY // 4 + 1)
    begin = jax.random.randint(keys[2], (), 0, NY - span + 1)
    xcell = jnp.arange(NX, dtype=jnp.int32)[:, None]
    ycell = jnp.arange(NY, dtype=jnp.int32)[None, :]
    in_x = (xcell == layer) | (xcell == (layer + 1) % NX)
    in_y = (ycell >= begin) & (ycell < begin + span)
    return (in_x & in_y).astype(jnp.int32)


def setup_inputs(seed: int = 0) -> dict:
    arg_keys = jax.random.split(jax.random.key(seed), 3)
    distribution = draw_distribution(jax.random.fold_in(arg_keys[2], 71), 0)
    wall_mask = draw_wall_mask(jax.random.fold_in(arg_keys[2], 71), 0)
    return {"distribution": distribution, "wall_mask": wall_mask}


half_span = 4.5
step_ratio = 0.1
knudsen = 0.5
prandtl = 2.0 / 3.0
omega_exp = 0.81
dens_floor = 0.1
temp_floor = 0.1


def velocity_nodes(first, count, nodes):
    index = first + jnp.arange(count, dtype=jnp.int32)
    total = nodes ** 3
    plane = nodes * nodes
    upper = index >= total // 2
    folded = jnp.where(upper, total - 1 - index, index)
    xcell = folded // plane
    xcell = jnp.where(upper, nodes - 1 - xcell, xcell)
    rest = folded % plane
    ycell = rest // nodes
    zcell = rest % nodes
    spacing = 2.0 * half_span / nodes
    return tuple((cell.astype(jnp.float32) + 0.5) * spacing - half_span for cell in (xcell, ycell, zcell))


def moment_table(vx, vy, vz, nodes):
    weight = (2.0 * half_span / nodes) ** 3 / (2.0 * math.pi) ** 1.5
    square = vx * vx + vy * vy + vz * vz
    rows = [jnp.ones_like(vx), vx, vy, vz, vx * vx, vy * vy, vz * vz, vx * vy, vx * vz, vy * vz,
            vx * square, vy * square, vz * square]
    return jnp.stack(rows) * weight


def upwind(field, speed, axis):
    back_one = jnp.roll(field, 1, axis)
    back_two = jnp.roll(field, 2, axis)
    fore_one = jnp.roll(field, -1, axis)
    fore_two = jnp.roll(field, -2, axis)
    plus = 0.5 * (3.0 * field - 4.0 * back_one + back_two)
    minus = -0.5 * (3.0 * field - 4.0 * fore_one + fore_two)
    return speed * jnp.where(speed > 0, plus, minus)


def shakhov_params(moments):
    raw = moments[0]
    density = jnp.maximum(raw, dens_floor)
    mx, my, mz = moments[1], moments[2], moments[3]
    ux, uy, uz = mx / density, my / density, mz / density
    sxx, syy, szz = moments[4], moments[5], moments[6]
    sxy, sxz, syz = moments[7], moments[8], moments[9]
    energy = sxx + syy + szz
    speed2 = ux * ux + uy * uy + uz * uz
    temper = jnp.maximum((energy / density - speed2) / 3.0, temp_floor)
    along = ux * mx + uy * my + uz * mz

    def heat(third, first, uval, dot_row):
        return 0.5 * (third - 2.0 * dot_row + speed2 * first - uval * energy + 2.0 * uval * along - uval * speed2 * raw)

    qx = heat(moments[10], mx, ux, ux * sxx + uy * sxy + uz * sxz)
    qy = heat(moments[11], my, uy, ux * sxy + uy * syy + uz * syz)
    qz = heat(moments[12], mz, uz, ux * sxz + uy * syz + uz * szz)
    factor = step_ratio * density * temper ** (1.0 - omega_exp) / knudsen
    return jnp.stack([density, ux, uy, uz, temper, qx, qy, qz, factor])


def relax(field, params, vx, vy, vz):
    shape = (9,) + field.shape[1:]
    density, ux, uy, uz, temper, qx, qy, qz, factor = params.reshape(shape)
    cx = vx[:, None, None] - ux[None]
    cy = vy[:, None, None] - uy[None]
    cz = vz[:, None, None] - uz[None]
    square = cx * cx + cy * cy + cz * cz
    maxwell = density[None] * temper[None] ** -1.5 * jnp.exp(-square / (2.0 * temper[None]))
    flux = (cx * qx[None] + cy * qy[None] + cz * qz[None]) / (5.0 * density[None] * temper[None] * temper[None])
    shakhov = maxwell * (1.0 + (1.0 - prandtl) * flux * (square / temper[None] - 5.0))
    return field + factor[None] * (shakhov - field)


def reference(distribution, wall_mask):
    wall = wall_mask > 0
    blocks = N_VEL
    state = distribution
    for step in range(STEPS):
        def move(k):
            piece = lax.dynamic_slice_in_dim(state, k * VB, VB, 0)
            vx, vy, vz = velocity_nodes(k * VB, VB, NODES)
            return piece - step_ratio * (upwind(piece, vx[:, None, None], 1) + upwind(piece, vy[:, None, None], 2))

        def reflect(k):
            own = move(k)
            other = move(blocks - 1 - k)[::-1]
            result = jnp.where(wall[None], other, own)
            vx, vy, vz = velocity_nodes(k * VB, VB, NODES)
            part = jnp.dot(moment_table(vx, vy, vz, NODES), result.reshape(VB, -1),
                           precision=lax.Precision.HIGHEST, preferred_element_type=jnp.float32)
            return result, part

        reflected, parts = lax.map(reflect, jnp.arange(blocks, dtype=jnp.int32))
        params = shakhov_params(jnp.sum(parts, axis=0))

        def collide(k):
            vx, vy, vz = velocity_nodes(k * VB, VB, NODES)
            return relax(reflected[k], params, vx, vy, vz)

        state = lax.map(collide, jnp.arange(blocks, dtype=jnp.int32)).reshape(VEL, NX, NY)
    return state
```

```python
import functools
import math

import jax
import jax.numpy as jnp
from jax import lax
from jax.experimental import pallas as pl
from jax.experimental.pallas import tpu as pltpu
from jax.sharding import PartitionSpec as P

MESH = pl.DeviceIdType.MESH
SPACE = 16
VEL = 16
ROWS = 864
COLS = 4
LANES = 128
CHUNKS = 6
CROWS = ROWS // CHUNKS
NODE = 9.0 / 24.0
WEIGHT = NODE**3 / (2.0 * math.pi) ** 1.5
STEP = 0.1
F32 = jnp.float32


def signal(sem, device):
    pl.semaphore_signal(sem, inc=1, device_id=device, device_id_type=MESH)


def remote(src, dst, send, recv, device):
    return pltpu.make_async_remote_copy(
        src_ref=src, dst_ref=dst, send_sem=send, recv_sem=recv, device_id=device, device_id_type=MESH
    )


class Place:
    def __init__(self):
        self.s = lax.axis_index("space")
        self.v = lax.axis_index("vel")
        self.pos = self.v // 8
        ahead = self.pos * 2 - 1
        self.down = (lax.rem(self.s + ahead + SPACE, SPACE), self.v)
        self.up = (lax.rem(self.s - ahead + SPACE, SPACE), self.v)
        self.block = jnp.where(self.pos == 1, 15 - self.v, self.v)
        self.core = lax.rem(self.v, 2)
        self.chip = self.v // 2

    def layer(self, flow):
        return self.pos * (2 * flow - 3) + 3 - flow

    def group(self, g):
        index = 3 * self.block + jnp.where(self.pos == 1, 2 - g, g)
        half = lax.rem(index, 2)
        speed = 4.5 - ((index // 2).astype(F32) + 0.5) * NODE
        first = 12 * half + jnp.where(self.pos == 1, 11, 0)
        slope = (1 - 2 * self.pos).astype(F32) * NODE
        y0 = (first.astype(F32) + 0.5) * NODE - 4.5
        return speed, half, y0, slope

    def vx(self, speed):
        return speed * (2 * self.pos - 1).astype(F32)

    def z(self, t):
        sub = lax.broadcasted_iota(jnp.int32, (8, LANES), 0).astype(F32)
        return ((sub + (8 * t + 0.5)) * NODE - 4.5) * (1 - 2 * self.pos).astype(F32)


def at(row):
    return pl.ds(pl.multiple_of(row, 8), 8)


def transport(place, field, moved, flows, g, first, count):
    speed, half, y0, slope = place.group(g)
    shift = jnp.where(half == 1, 1, LANES - 1)
    alpha = STEP * speed

    def run(r, carry):
        beta = STEP * jnp.abs(y0 + slope * r.astype(F32))
        keep = 1.0 - 1.5 * (alpha + beta)
        for t in range(3):
            rows = at((g * 12 + r) * 24 + 8 * t)
            lines = {l: field[l, rows, :] for l in range(flows[0], flows[-1] + 3)}
            for l in flows:
                own = lines[l + 2]
                near = own - 0.25 * pltpu.roll(own, shift, 1)
                near = pltpu.roll(near, shift, 1)
                moved[l, rows, :] = (
                    keep * own
                    + (2.0 * alpha) * (lines[l + 1] - 0.25 * lines[l])
                    + (2.0 * beta) * near
                )
        return carry

    lax.fori_loop(first, first + count, run, 0)


def moments(place, field, part, sums, z_sums):
    def group(g, carry):
        speed, half, y0, slope = place.group(g)
        x = place.vx(speed)
        for t in range(3):

            def run(r, acc):
                y = y0 + slope * r.astype(F32)
                rows = at((g * 12 + r) * 24 + 8 * t)
                out = []
                for l in range(COLS):
                    f0 = field[l, rows, :]
                    f1 = y * f0
                    f2 = y * f1
                    f3 = y * f2
                    out += [acc[4 * l] + f0, acc[4 * l + 1] + f1, acc[4 * l + 2] + f2, acc[4 * l + 3] + f3]
                return tuple(out)

            acc = lax.fori_loop(0, 12, run, (jnp.zeros((8, LANES), F32),) * 16)
            z = place.z(t)
            for l in range(COLS):
                a, b, c, d = acc[4 * l : 4 * l + 4]
                za = z * a
                zb = z * b
                zza = z * za
                terms = [a, b, c, d, za, zb, z * c, zza, z * zb, z * zza]
                for m, term in enumerate(terms):
                    if t == 0:
                        z_sums[l, m] = term
                    else:
                        z_sums[l, m] = z_sums[l, m] + term
        for l in range(COLS):
            a, b, c, d, za, zb, zc, zza, zzb, zzza = [z_sums[l, m] for m in range(10)]
            xx = x * x
            rows13 = [
                a,
                x * a,
                b,
                za,
                xx * a,
                c,
                zza,
                x * b,
                x * za,
                zb,
                x * (xx * a + c + zza),
                xx * b + d + zzb,
                xx * za + zc + zzza,
            ]
            for m, value in enumerate(rows13):
                part[l, m] = part[l, m] + value
        return carry

    part[...] = jnp.zeros_like(part)
    lax.fori_loop(0, 3, group, 0)
    for l in range(COLS):
        rows = [jnp.sum(part[l, m], axis=0, keepdims=True) * WEIGHT for m in range(13)]
        sums[place.layer(l)] = jnp.concatenate(rows + [jnp.zeros((3, LANES), F32)], axis=0)


def cell_params(m):
    raw = m[0]
    density = jnp.maximum(raw, 0.1)
    mx, my, mz = m[1], m[2], m[3]
    inv = 1.0 / density
    ux, uy, uz = mx * inv, my * inv, mz * inv
    sxx, syy, szz, sxy, sxz, syz = m[4:10]
    energy = sxx + syy + szz
    speed2 = ux * ux + uy * uy + uz * uz
    temper = jnp.maximum((energy * inv - speed2) / 3.0, 0.1)
    along = ux * mx + uy * my + uz * mz

    def heat(third, first, uval, dot_row):
        return 0.5 * (
            third
            - 2.0 * dot_row
            + speed2 * first
            - uval * energy
            + 2.0 * uval * along
            - uval * speed2 * raw
        )

    qx = heat(m[10], mx, ux, ux * sxx + uy * sxy + uz * sxz)
    qy = heat(m[11], my, uy, ux * sxy + uy * syy + uz * syz)
    qz = heat(m[12], mz, uz, ux * sxz + uy * syz + uz * szz)
    factor = (STEP / 0.5) * density * jnp.exp(0.19 * jnp.log(temper))
    inv_t = 1.0 / temper
    scale = (1.0 - 2.0 / 3.0) / (5.0 * density * temper * temper)
    peak = density * inv_t * lax.rsqrt(temper)
    return [ux, uy, uz, 0.5 * inv_t, inv_t, peak * factor, scale * qx, scale * qy, scale * qz, 1.0 - factor]


def spread(row):
    return jnp.broadcast_to(row, (8, LANES))


def relax(place, load, store, params, p, table):
    ux, uy, uz, half_t, inv_t, peak, kx, ky, kz, keep = [params[p, pl.ds(i, 1), :] for i in range(10)]
    z_exp, z_dot, z_square = [], [], []
    for t in range(3):
        c = place.z(t) - spread(uz)
        z_exp.append(jnp.exp(-(c * c) * spread(half_t)))
        z_dot.append(c * spread(kz))
        z_square.append(c * c * spread(inv_t))
    keep8 = spread(keep)
    for g in range(3):
        speed, half, y0, slope = place.group(g)
        cx = place.vx(speed) - ux
        for part in range(2):
            index = lax.broadcasted_iota(jnp.int32, (8, LANES), 0).astype(F32) + 8.0 * part
            cy = (y0 + slope * index) - spread(uy)
            square = spread(cx * cx) + cy * cy
            rows = pl.ds(16 * g + 8 * part, 8)
            table[0, rows, :] = spread(peak) * jnp.exp(-square * spread(half_t))
            table[1, rows, :] = spread(cx * kx) + cy * spread(ky)
            table[2, rows, :] = square * spread(inv_t) - 5.0
    for g in range(3):

        def run(r, carry):
            line = pl.ds(16 * g + r, 1)
            amp = spread(table[0, line, :])
            dot = spread(table[1, line, :])
            square = spread(table[2, line, :])
            for t in range(3):
                row = (g * 12 + r) * 24 + 8 * t
                old = load(row)
                shape = 1.0 + (dot + z_dot[t]) * (square + z_square[t])
                store(row, keep8 * old + (amp * z_exp[t]) * shape)
            return carry

        lax.fori_loop(0, 12, run, 0, unroll=2)


def flip8(x):
    sub = lax.broadcasted_iota(jnp.int32, (8, LANES), 0)
    x = pltpu.roll(x, 4, 0)
    x = jnp.where(sub % 4 < 2, pltpu.roll(x, 6, 0), pltpu.roll(x, 2, 0))
    return jnp.where(sub % 2 < 1, pltpu.roll(x, 7, 0), pltpu.roll(x, 1, 0))


def first_kernel(x_ref, mask_ref, moved, walls, where, raw, field, note, hear, in_sem, ssem, rsem, nsem, hsem):
    place = Place()
    s, v = place.s, place.v
    span = CROWS * COLS
    loads = [
        pltpu.make_async_copy(x_ref.at[pl.ds(c * span, span)], raw.at[pl.ds(c * span, span)], in_sem.at[c])
        for c in range(CHUNKS)
    ]
    for copy in loads:
        copy.start()

    line, z = s // 4, lax.rem(s, 4)
    mates = [(line * 4 + lax.rem(z + i, 4), v) for i in range(1, 4)]
    cross = [(lax.rem(line + i, 4) * 4 + z, v) for i in range(1, 4)]
    barrier = pltpu.get_barrier_semaphore()
    for device in [place.up] + mates + cross:
        signal(barrier, device)

    mask = mask_ref[...].astype(F32)
    has = [jnp.broadcast_to(jnp.max(mask[i : i + 1, :], axis=1, keepdims=True), (1, LANES)) for i in range(COLS)]
    first = has[0]
    second = (1.0 - has[0]) * has[1]
    walls[0:4, :] = mask
    walls[4:8, :] = jnp.concatenate([first, second, 1.0 - first - second, jnp.zeros_like(first)], axis=0)
    here = jnp.maximum(jnp.maximum(has[1], has[2]), has[3]) * s.astype(F32)
    note[0] = spread(here)

    def split(flows, c):
        def body(i, carry):
            row = c * CROWS + 8 * i
            for l in flows:
                field[l + 2, at(row), :] = raw[pl.ds(row * COLS + place.layer(l), 8, stride=COLS), :]
            return carry

        lax.fori_loop(0, CROWS // 8, body, 0, unroll=2)

    sends = []
    for c in range(CHUNKS):
        loads[c].wait()
        split((2, 3), c)
        if c == 0:
            pl.semaphore_wait(barrier, 7)
        rows = pl.ds(c * CROWS, CROWS)
        copy = remote(
            field.at[pl.ds(4, 2), rows], field.at[pl.ds(0, 2), rows], ssem.at[c], rsem.at[c], place.down
        )
        copy.start()
        sends.append(copy)
    words = [remote(note.at[0], hear.at[i], nsem.at[i], hsem.at[i], mates[i]) for i in range(3)]
    for copy in words:
        copy.start()
    for c in range(CHUNKS):
        split((0, 1), c)
    for copy in words:
        copy.wait_recv()
    note[1] = note[0] + hear[0] + hear[1] + hear[2]
    more = [remote(note.at[1], hear.at[3 + i], nsem.at[3 + i], hsem.at[3 + i], cross[i]) for i in range(3)]
    for copy in more:
        copy.start()

    def later(g, carry):
        transport(place, field, moved, (2, 3), g, 0, 12)
        return carry

    lax.fori_loop(0, 3, later, 0)
    for copy in more:
        copy.wait_recv()
    total = note[1] + hear[3] + hear[4] + hear[5]
    where[0] = jnp.max(total).astype(jnp.int32)
    for c in range(CHUNKS):
        sends[c].wait_recv()
        transport(place, field, moved, (0, 1), c // 2, 6 * (c % 2), 6)
    for copy in sends + words + more:
        copy.wait_send()


def second_kernel(
    block,
    moved_ref,
    walls,
    out,
    one,
    halo,
    field,
    two,
    slab,
    mirror,
    part,
    z_sums,
    sums,
    swap,
    gather,
    params,
    edge,
    table,
    in_sem,
    hsem,
    xsem,
    psem,
    esem,
):
    place = Place()
    s, v = place.s, place.v
    load = pltpu.make_async_copy(moved_ref, one, in_sem)
    load.start()
    after = (block + 1) % SPACE
    near_wall = jnp.logical_or(s == block, s == after)
    partner = (s, 15 - v)
    peer = (s, v + 1 - 2 * place.core)
    chips = [lax.rem(place.chip + i, 8) for i in range(1, 8)]
    mates = [(s, 2 * chip + place.core) for chip in chips]

    barrier = pltpu.get_barrier_semaphore()
    for device in [place.up, peer] + mates:
        signal(barrier, device)

    @pl.when(near_wall)
    def _():
        signal(barrier, partner)
        pl.semaphore_wait(barrier, 10)

    @pl.when(jnp.logical_not(near_wall))
    def _():
        pl.semaphore_wait(barrier, 9)

    load.wait()

    def reflect(state, k):
        def cut(i, carry):
            rows = at(8 * i)
            lines = [state[place.layer(l), rows, :] for l in range(COLS)]
            at0 = spread(walls[4:5, :]) > 0.5
            at1 = spread(walls[5:6, :]) > 0.5
            slab[k, 0, rows, :] = jnp.where(at0, lines[0], jnp.where(at1, lines[1], lines[2]))
            slab[k, 1, rows, :] = jnp.where(at0, lines[1], jnp.where(at1, lines[2], lines[3]))
            return carry

        def put(i, carry):
            rows = at(8 * i)
            back = at(ROWS - 8 - 8 * i)
            near = flip8(mirror[k, 0, back, :])
            far = flip8(mirror[k, 1, back, :])
            for l in range(COLS):
                new = jnp.where(spread(walls[4 + l : 5 + l, :]) > 0.5, near, far)
                line = place.layer(l)
                state[line, rows, :] = jnp.where(spread(walls[l : l + 1, :]) > 0.5, new, state[line, rows, :])
            return carry

        @pl.when(s == block)
        def _():
            lax.fori_loop(0, ROWS // 8, cut, 0)
            copy = remote(slab.at[k], mirror.at[k], xsem.at[k, 0], xsem.at[k, 1], partner)
            copy.start()
            copy.wait()
            lax.fori_loop(0, ROWS // 8, put, 0)

        @pl.when(s == after)
        def _():
            lax.fori_loop(0, ROWS // 8, cut, 0)
            mirror[k, 1] = jnp.zeros((ROWS, LANES), F32)
            copy = remote(slab.at[k, 0], mirror.at[k, 0], xsem.at[k, 0], xsem.at[k, 1], partner)
            copy.start()
            copy.wait()
            lax.fori_loop(0, ROWS // 8, put, 0)

    def total(k):
        mine = pl.ds(2 * place.core, 2)
        first = remote(
            sums.at[k, pl.ds(2 - 2 * place.core, 2)], swap.at[k], psem.at[k, 0, 0], psem.at[k, 1, 0], peer
        )
        first.start()
        first.wait_recv()
        gather[k, place.chip] = sums[k, mine] + swap[k]
        outs = []
        for i, mate in enumerate(mates):
            copy = remote(
                gather.at[k, place.chip], gather.at[k, place.chip], psem.at[k, 0, i + 1], psem.at[k, 1, i + 1], mate
            )
            copy.start()
            outs.append(copy)
        for copy in outs:
            copy.wait_recv()
        whole = gather[k, 0]
        for i in range(1, 8):
            whole = whole + gather[k, i]
        rows = cell_params([whole[:, i, :] for i in range(13)])
        for i, row in enumerate(rows):
            params[k, mine, i, :] = row
        last = remote(params.at[k, mine], params.at[k, mine], psem.at[k, 0, 8], psem.at[k, 1, 8], peer)
        last.start()
        last.wait_recv()
        return [first, last] + outs

    reflect(one, 0)
    hand = remote(one.at[pl.ds(2, 2)], halo, hsem.at[0], hsem.at[1], place.down)
    hand.start()
    moments(place, one, part, sums.at[0], z_sums)
    open_copies = total(0)
    tell = remote(
        params.at[0, pl.ds(2 * place.pos, 2)], edge, esem.at[0], esem.at[1], place.down
    )
    tell.start()

    def own(l, carry):
        def load_row(row):
            return one[l, at(row), :]

        def store_row(row, value):
            field[l + 2, at(row), :] = value

        relax(place, load_row, store_row, params.at[0], place.layer(l), table)
        return carry

    lax.fori_loop(0, COLS, own, 0)
    tell.wait_recv()
    hand.wait_recv()

    def beside(l, carry):
        def load_row(row):
            return halo[l, at(row), :]

        def store_row(row, value):
            field[l, at(row), :] = value

        relax(place, load_row, store_row, edge, jnp.where(place.pos == 1, l, 1 - l), table)
        return carry

    lax.fori_loop(0, 2, beside, 0)

    def step(g, carry):
        transport(place, field, two, (0, 1, 2, 3), g, 0, 12)
        return carry

    lax.fori_loop(0, 3, step, 0)

    reflect(two, 1)
    moments(place, two, part, sums.at[1], z_sums)
    open_copies += total(1)

    def end(l, carry):
        layer = place.layer(l)

        def load_row(row):
            return two[l, at(row), :]

        def store_row(row, value):
            out[pl.ds(row * COLS + layer, 8, stride=COLS), :] = value

        relax(place, load_row, store_row, params.at[1], layer, table)
        return carry

    lax.fori_loop(0, COLS, end, 0)
    for copy in open_copies + [hand, tell]:
        copy.wait_send()


def first_call(x, mask):
    dma = pltpu.SemaphoreType.DMA
    return pl.pallas_call(
        first_kernel,
        out_shape=(
            jax.ShapeDtypeStruct((COLS, ROWS, LANES), F32),
            jax.ShapeDtypeStruct((8, LANES), F32),
            jax.ShapeDtypeStruct((1,), jnp.int32),
        ),
        in_specs=[pl.BlockSpec(memory_space=pl.ANY), pl.BlockSpec(memory_space=pltpu.VMEM)],
        out_specs=(
            pl.BlockSpec(memory_space=pltpu.VMEM),
            pl.BlockSpec(memory_space=pltpu.VMEM),
            pl.BlockSpec(memory_space=pltpu.SMEM),
        ),
        scratch_shapes=[
            pltpu.VMEM((ROWS * COLS, LANES), F32),
            pltpu.VMEM((COLS + 2, ROWS, LANES), F32),
            pltpu.VMEM((2, 8, LANES), F32),
            pltpu.VMEM((6, 8, LANES), F32),
            dma((CHUNKS,)),
            dma((CHUNKS,)),
            dma((CHUNKS,)),
            dma((6,)),
            dma((6,)),
        ],
        compiler_params=pltpu.CompilerParams(
            collective_id=0, has_side_effects=True, vmem_limit_bytes=24 << 20
        ),
        name="first",
    )(x, mask)


def second_call(block, moved, walls):
    dma = pltpu.SemaphoreType.DMA
    return pl.pallas_call(
        functools.partial(second_kernel, block),
        out_shape=jax.ShapeDtypeStruct((ROWS * COLS, LANES), F32),
        in_specs=[pl.BlockSpec(memory_space=pl.ANY), pl.BlockSpec(memory_space=pltpu.VMEM)],
        out_specs=pl.BlockSpec(memory_space=pltpu.VMEM),
        scratch_shapes=[
            pltpu.VMEM((COLS, ROWS, LANES), F32),
            pltpu.VMEM((2, ROWS, LANES), F32),
            pltpu.VMEM((COLS + 2, ROWS, LANES), F32),
            pltpu.VMEM((COLS, ROWS, LANES), F32),
            pltpu.VMEM((2, 2, ROWS, LANES), F32),
            pltpu.VMEM((2, 2, ROWS, LANES), F32),
            pltpu.VMEM((COLS, 13, 8, LANES), F32),
            pltpu.VMEM((COLS, 10, 8, LANES), F32),
            pltpu.VMEM((2, COLS, 16, LANES), F32),
            pltpu.VMEM((2, 2, 16, LANES), F32),
            pltpu.VMEM((2, 8, 2, 16, LANES), F32),
            pltpu.VMEM((2, COLS, 16, LANES), F32),
            pltpu.VMEM((2, 16, LANES), F32),
            pltpu.VMEM((3, 48, LANES), F32),
            dma,
            dma((2,)),
            dma((2, 2)),
            dma((2, 2, 9)),
            dma((2,)),
        ],
        compiler_params=pltpu.CompilerParams(
            collective_id=1 + block, has_side_effects=True, vmem_limit_bytes=32 << 20
        ),
        name=f"second{block}",
    )(moved, walls)


def shards(distribution, wall_mask):
    x = distribution.reshape(ROWS * COLS, LANES)
    moved, walls, where = first_call(x, wall_mask)
    branches = [functools.partial(second_call, block) for block in range(SPACE)]
    out = lax.switch(where[0], branches, moved, walls)
    return out.reshape(distribution.shape)


def solution(mesh):
    placed = (P("vel", "space", None), P("space", None))
    return jax.shard_map(
        shards, mesh=mesh, in_specs=placed, out_specs=P("vel", "space", None), check_vma=False
    )
```

```python
import functools
import math

import jax
import jax.numpy as jnp
from jax import lax
from jax.experimental import pallas as pl
from jax.experimental.pallas import tpu as pltpu
from jax.sharding import PartitionSpec as P

MESH = pl.DeviceIdType.MESH
SPACE = 16
VEL = 16
ROWS = 864
COLS = 4
LANES = 128
CHUNKS = 6
CROWS = ROWS // CHUNKS
NODE = 9.0 / 24.0
WEIGHT = NODE**3 / (2.0 * math.pi) ** 1.5
STEP = 0.1
F32 = jnp.float32


def signal(sem, device):
    pl.semaphore_signal(sem, inc=1, device_id=device, device_id_type=MESH)


def remote(src, dst, send, recv, device):
    return pltpu.make_async_remote_copy(
        src_ref=src, dst_ref=dst, send_sem=send, recv_sem=recv, device_id=device, device_id_type=MESH
    )


class Place:
    def __init__(self):
        self.s = lax.axis_index("space")
        self.v = lax.axis_index("vel")
        self.pos = self.v // 8
        ahead = self.pos * 2 - 1
        self.down = (lax.rem(self.s + ahead + SPACE, SPACE), self.v)
        self.up = (lax.rem(self.s - ahead + SPACE, SPACE), self.v)
        self.block = jnp.where(self.pos == 1, 15 - self.v, self.v)
        self.core = lax.rem(self.v, 2)
        self.chip = self.v // 2

    def layer(self, flow):
        return self.pos * (2 * flow - 3) + 3 - flow

    def group(self, g):
        index = 3 * self.block + jnp.where(self.pos == 1, 2 - g, g)
        half = lax.rem(index, 2)
        speed = 4.5 - ((index // 2).astype(F32) + 0.5) * NODE
        first = 12 * half + jnp.where(self.pos == 1, 11, 0)
        slope = (1 - 2 * self.pos).astype(F32) * NODE
        y0 = (first.astype(F32) + 0.5) * NODE - 4.5
        return speed, half, y0, slope

    def vx(self, speed):
        return speed * (2 * self.pos - 1).astype(F32)

    def z(self, t):
        sub = lax.broadcasted_iota(jnp.int32, (8, LANES), 0).astype(F32)
        return ((sub + 8.0 * jnp.asarray(t, F32) + 0.5) * NODE - 4.5) * (1 - 2 * self.pos).astype(F32)


def at(row):
    return pl.ds(pl.multiple_of(row, 8), 8)


def transport(place, field, moved, flows, g, first, count):
    speed, half, y0, slope = place.group(g)
    shift = jnp.where(half == 1, 1, LANES - 1)
    alpha = STEP * speed

    def run(r, carry):
        beta = STEP * jnp.abs(y0 + slope * r.astype(F32))
        keep = 1.0 - 1.5 * (alpha + beta)
        for t in range(3):
            rows = at((g * 12 + r) * 24 + 8 * t)
            lines = {l: field[l, rows, :] for l in range(flows[0], flows[-1] + 3)}
            nears = {l: lines[l + 2] - 0.25 * pltpu.roll(lines[l + 2], shift, 1) for l in flows}
            nears = {l: pltpu.roll(nears[l], shift, 1) for l in flows}
            for l in flows:
                moved[l, rows, :] = (
                    keep * lines[l + 2]
                    + (2.0 * alpha) * (lines[l + 1] - 0.25 * lines[l])
                    + (2.0 * beta) * nears[l]
                )
        return carry

    lax.fori_loop(first, first + count, run, 0, unroll=6)


def moments(place, field, part, sums, z_sums):
    def group(g, carry):
        speed, half, y0, slope = place.group(g)
        x = place.vx(speed)
        z_sums[...] = jnp.zeros_like(z_sums)

        def tile(t, carry):
            def run(r, acc):
                y = y0 + slope * r.astype(F32)
                rows = at((g * 12 + r) * 24 + 8 * t)
                out = []
                for l in range(COLS):
                    f0 = field[l, rows, :]
                    f1 = y * f0
                    f2 = y * f1
                    f3 = y * f2
                    out += [acc[4 * l] + f0, acc[4 * l + 1] + f1, acc[4 * l + 2] + f2, acc[4 * l + 3] + f3]
                return tuple(out)

            acc = lax.fori_loop(0, 12, run, (jnp.zeros((8, LANES), F32),) * 16, unroll=12)
            z = place.z(t)
            for l in range(COLS):
                a, b, c, d = acc[4 * l : 4 * l + 4]
                za = z * a
                zb = z * b
                zza = z * za
                for m, term in enumerate([a, b, c, d, za, zb, z * c, zza, z * zb, z * zza]):
                    z_sums[l, m] = z_sums[l, m] + term
            return carry

        lax.fori_loop(0, 3, tile, 0)
        for l in range(COLS):
            a, b, c, d, za, zb, zc, zza, zzb, zzza = [z_sums[l, m] for m in range(10)]
            xx = x * x
            rows13 = [
                a,
                x * a,
                b,
                za,
                xx * a,
                c,
                zza,
                x * b,
                x * za,
                zb,
                x * (xx * a + c + zza),
                xx * b + d + zzb,
                xx * za + zc + zzza,
            ]
            for m, value in enumerate(rows13):
                part[l, m] = part[l, m] + value
        return carry

    part[...] = jnp.zeros_like(part)
    lax.fori_loop(0, 3, group, 0)
    for l in range(COLS):
        rows = [jnp.sum(part[l, m], axis=0, keepdims=True) * WEIGHT for m in range(13)]
        sums[place.layer(l)] = jnp.concatenate(rows + [jnp.zeros((3, LANES), F32)], axis=0)


def cell_params(m):
    raw = m[0]
    density = jnp.maximum(raw, 0.1)
    mx, my, mz = m[1], m[2], m[3]
    inv = 1.0 / density
    ux, uy, uz = mx * inv, my * inv, mz * inv
    sxx, syy, szz, sxy, sxz, syz = m[4:10]
    energy = sxx + syy + szz
    speed2 = ux * ux + uy * uy + uz * uz
    temper = jnp.maximum((energy * inv - speed2) / 3.0, 0.1)
    along = ux * mx + uy * my + uz * mz

    def heat(third, first, uval, dot_row):
        return 0.5 * (
            third
            - 2.0 * dot_row
            + speed2 * first
            - uval * energy
            + 2.0 * uval * along
            - uval * speed2 * raw
        )

    qx = heat(m[10], mx, ux, ux * sxx + uy * sxy + uz * sxz)
    qy = heat(m[11], my, uy, ux * sxy + uy * syy + uz * syz)
    qz = heat(m[12], mz, uz, ux * sxz + uy * syz + uz * szz)
    factor = (STEP / 0.5) * density * jnp.exp(0.19 * jnp.log(temper))
    inv_t = 1.0 / temper
    scale = (1.0 - 2.0 / 3.0) / (5.0 * density * temper * temper)
    peak = density * inv_t * lax.rsqrt(temper)
    return [ux, uy, uz, 0.5 * inv_t, inv_t, peak * factor, scale * qx, scale * qy, scale * qz, 1.0 - factor]


def spread(row):
    return jnp.broadcast_to(row, (8, LANES))


def relax(place, load, store, params, p, table, groups=(0, 3)):
    ux, uy, uz, half_t, inv_t, peak, kx, ky, kz, keep = [params[p, pl.ds(i, 1), :] for i in range(10)]
    z_exp, z_dot, z_square = [], [], []
    for t in range(3):
        c = place.z(t) - spread(uz)
        z_exp.append(jnp.exp(-(c * c) * spread(half_t)))
        z_dot.append(c * spread(kz))
        z_square.append(c * c * spread(inv_t))
    keep8 = spread(keep)
    def group(g, carry):
        speed, half, y0, slope = place.group(g)
        cx = place.vx(speed) - ux
        for part in range(2):
            index = lax.broadcasted_iota(jnp.int32, (8, LANES), 0).astype(F32) + 8.0 * part
            cy = (y0 + slope * index) - spread(uy)
            square = spread(cx * cx) + cy * cy
            rows = pl.ds(8 * part, 8)
            table[0, rows, :] = spread(peak) * jnp.exp(-square * spread(half_t))
            table[1, rows, :] = spread(cx * kx) + cy * spread(ky)
            table[2, rows, :] = square * spread(inv_t) - 5.0

        def run(r, carry):
            line = pl.ds(r, 1)
            amp = spread(table[0, line, :])
            dot = spread(table[1, line, :])
            square = spread(table[2, line, :])
            for t in range(3):
                row = (g * 12 + r) * 24 + 8 * t
                old = load(row)
                shape = 1.0 + (dot + z_dot[t]) * (square + z_square[t])
                store(row, keep8 * old + (amp * z_exp[t]) * shape)
            return carry

        return lax.fori_loop(0, 12, run, carry, unroll=12)

    lax.fori_loop(groups[0], groups[1], group, 0)


def flip8(x):
    sub = lax.broadcasted_iota(jnp.int32, (8, LANES), 0)
    x = pltpu.roll(x, 4, 0)
    x = jnp.where(sub % 4 < 2, pltpu.roll(x, 6, 0), pltpu.roll(x, 2, 0))
    return jnp.where(sub % 2 < 1, pltpu.roll(x, 7, 0), pltpu.roll(x, 1, 0))


def first_kernel(
    x_ref, mask_ref, moved, walls, where, raw, mask_in, field, note, hear, in_sem, mask_sem, ssem, rsem, nsem, hsem
):
    place = Place()
    s, v = place.s, place.v
    span = CROWS * COLS
    mask_copy = pltpu.make_async_copy(mask_ref, mask_in, mask_sem)
    mask_copy.start()
    loads = [
        pltpu.make_async_copy(x_ref.at[pl.ds(c * span, span)], raw.at[pl.ds(c * span, span)], in_sem.at[c])
        for c in range(CHUNKS)
    ]
    for copy in loads:
        copy.start()

    line, z = s // 4, lax.rem(s, 4)
    mates = [(line * 4 + lax.rem(z + i, 4), v) for i in range(1, 4)]
    cross = [(lax.rem(line + i, 4) * 4 + z, v) for i in range(1, 4)]
    barrier = pltpu.get_barrier_semaphore()
    for device in [place.up] + mates + cross:
        signal(barrier, device)

    mask_copy.wait()
    mask = mask_in[...].astype(F32)
    has = [jnp.broadcast_to(jnp.max(mask[i : i + 1, :], axis=1, keepdims=True), (1, LANES)) for i in range(COLS)]
    first = has[0]
    second = (1.0 - has[0]) * has[1]
    walls[0:4, :] = mask
    walls[4:8, :] = jnp.concatenate([first, second, 1.0 - first - second, jnp.zeros_like(first)], axis=0)
    here = jnp.maximum(jnp.maximum(has[1], has[2]), has[3]) * s.astype(F32)
    note[0] = spread(here)

    def split(flows, c):
        def body(i, carry):
            row = c * CROWS + 8 * i
            for l in flows:
                field[l + 2, at(row), :] = raw[pl.ds(row * COLS + place.layer(l), 8, stride=COLS), :]
            return carry

        lax.fori_loop(0, CROWS // 8, body, 0, unroll=6)

    words = [remote(note.at[0], hear.at[i], nsem.at[i], hsem.at[i], mates[i]) for i in range(3)]
    sends = []
    for c in range(CHUNKS):
        loads[c].wait()
        split((2, 3), c)
        if c == 0:
            pl.semaphore_wait(barrier, 7)
            for copy in words:
                copy.start()
        rows = pl.ds(c * CROWS, CROWS)
        copy = remote(
            field.at[pl.ds(4, 2), rows], field.at[pl.ds(0, 2), rows], ssem.at[c], rsem.at[c], place.down
        )
        copy.start()
        sends.append(copy)
    for c in range(CHUNKS):
        split((0, 1), c)
    for copy in words:
        copy.wait_recv()
    note[1] = note[0] + hear[0] + hear[1] + hear[2]
    more = [remote(note.at[1], hear.at[3 + i], nsem.at[3 + i], hsem.at[3 + i], cross[i]) for i in range(3)]
    for copy in more:
        copy.start()

    def later(g, carry):
        transport(place, field, moved, (2, 3), g, 0, 12)
        return carry

    lax.fori_loop(0, 3, later, 0)
    for c in range(CHUNKS):
        sends[c].wait_recv()
        transport(place, field, moved, (0, 1), c // 2, 6 * (c % 2), 6)
    for copy in more:
        copy.wait_recv()
    total = note[1] + hear[3] + hear[4] + hear[5]
    where[0] = jnp.max(total).astype(jnp.int32)
    for copy in sends + words + more:
        copy.wait_send()


def second_kernel(
    block,
    moved_ref,
    walls,
    out,
    states,
    halo,
    field,
    slab,
    mirror,
    relay,
    part,
    z_sums,
    sums,
    swap,
    gather,
    params,
    edge,
    table,
    in_sem,
    halo_sem,
    out_sem,
    back_sem,
    relay_sem,
    pass_sem,
    psem,
    esem,
):
    place = Place()
    s, v = place.s, place.v
    load = pltpu.make_async_copy(moved_ref, states.at[0], in_sem)
    load.start()
    after = (block + 1) % SPACE
    sides = ((block + 4) % SPACE, (block + 12) % SPACE)
    beyond = (after + (8 if block % 4 < 3 else 4)) % SPACE
    in_block, in_after, in_beyond = s == block, s == after, s == beyond
    in_sides = jnp.logical_or(s == sides[0], s == sides[1])
    one_more = jnp.logical_or(in_sides, jnp.logical_or(in_after, in_beyond))
    partner = (s, 15 - v)
    peer = (s, v + 1 - 2 * place.core)
    chips = [lax.rem(place.chip + i, 8) for i in range(1, 8)]
    mates = [(s, 2 * chip + place.core) for chip in chips]

    barrier = pltpu.get_barrier_semaphore()
    for device in [place.up, peer] + mates:
        signal(barrier, device)

    @pl.when(in_block)
    def _():
        for device in [partner, (sides[0], 15 - v), (sides[1], 15 - v)]:
            signal(barrier, device)
        pl.semaphore_wait(barrier, 12)

    @pl.when(one_more)
    def _():
        source = jnp.where(in_sides, block, jnp.where(in_after, beyond, after))
        signal(barrier, (source, jnp.where(in_after, 15 - v, v)))
        pl.semaphore_wait(barrier, 10)

    @pl.when(jnp.logical_not(jnp.logical_or(in_block, one_more)))
    def _():
        pl.semaphore_wait(barrier, 9)

    load.wait()

    def reflect(state, k):
        def cut(i, carry):
            rows = at(8 * i)
            lines = [state[place.layer(l), rows, :] for l in range(COLS)]
            at0 = spread(walls[4:5, :]) > 0.5
            at1 = spread(walls[5:6, :]) > 0.5
            slab[k, 0, rows, :] = jnp.where(at0, lines[0], jnp.where(at1, lines[1], lines[2]))
            slab[k, 1, rows, :] = jnp.where(at0, lines[1], jnp.where(at1, lines[2], lines[3]))
            return carry

        def put(first, count):
            def body(i, carry):
                back = at(first + 8 * i)
                rows = at(ROWS - 8 - first - 8 * i)
                near = flip8(mirror[k, 0, back, :])
                far = flip8(mirror[k, 1, back, :])
                for l in range(COLS):
                    new = jnp.where(spread(walls[4 + l : 5 + l, :]) > 0.5, near, far)
                    line = place.layer(l)
                    state[line, rows, :] = jnp.where(spread(walls[l : l + 1, :]) > 0.5, new, state[line, rows, :])
                return carry

            lax.fori_loop(0, count // 8, body, 0, unroll=3)

        def direct(c):
            rows = pl.ds(96 * c, 96)
            return remote(
                slab.at[k, :, rows], mirror.at[k, :, rows], out_sem.at[k, c], back_sem.at[k, c], partner
            )

        def lead(side, c):
            rows = pl.ds(288 * (side + 1) + 96 * c, 96)
            return remote(
                slab.at[k, :, rows],
                relay.at[k, :, pl.ds(96 * c, 96)],
                out_sem.at[k, 3 * side + 3 + c],
                relay_sem.at[k, c],
                (sides[side], v),
            )

        def follow(side, c):
            rows = pl.ds(288 * (side + 1) + 96 * c, 96)
            return remote(
                relay.at[k, :, pl.ds(96 * c, 96)],
                mirror.at[k, :, rows],
                pass_sem.at[k, c],
                back_sem.at[k, 3 * side + 3 + c],
                (block, 15 - v),
            )

        def lead_far(c):
            return remote(
                slab.at[k, 0, pl.ds(288 * c, 288)],
                relay.at[k, c // 2, pl.ds(288 * (c % 2), 288)],
                out_sem.at[k, c],
                relay_sem.at[k, c],
                (beyond, v),
            )

        def follow_far(c):
            return remote(
                relay.at[k, c // 2, pl.ds(288 * (c % 2), 288)],
                mirror.at[k, 0, pl.ds(288 * c, 288)],
                pass_sem.at[k, c],
                back_sem.at[k, c],
                (after, 15 - v),
            )

        @pl.when(in_block)
        def _():
            def depart(c, carry):
                def each(side, carry):
                    first = 36 * side + 12 * c
                    return lax.fori_loop(0, 12, lambda i, carry: cut(first + i, carry), carry, unroll=3)

                lax.fori_loop(0, 3, each, carry)
                lead(0, c).start()
                lead(1, c).start()
                direct(c).start()
                return carry

            lax.fori_loop(0, 3, depart, 0)
            def arrive(c, carry):
                for side in range(3):
                    (follow(side - 1, c) if side else direct(c)).wait_recv()

                def each(side, carry):
                    put(288 * side + 96 * c, 96)
                    return carry

                return lax.fori_loop(0, 3, each, carry)

            lax.fori_loop(0, 3, arrive, 0)
            for c in range(3):
                direct(c).wait_send()
                lead(0, c).wait_send()
                lead(1, c).wait_send()

        for side in range(2):

            @pl.when(s == sides[side])
            def _():
                for c in range(3):
                    lead(side, c).wait_recv()
                    follow(side, c).start()
                for c in range(3):
                    follow(side, c).wait_send()

        @pl.when(in_after)
        def _():
            mirror[k, 1] = jnp.zeros((ROWS, LANES), F32)
            lax.fori_loop(0, ROWS // 8, cut, 0, unroll=3)
            for c in range(3):
                lead_far(c).start()
            for c in range(3):
                follow_far(c).wait_recv()
            put(0, ROWS)
            for c in range(3):
                lead_far(c).wait_send()

        @pl.when(in_beyond)
        def _():
            for c in range(3):
                lead_far(c).wait_recv()
                follow_far(c).start()
            for c in range(3):
                follow_far(c).wait_send()

    def total(k, between):
        mine = pl.ds(2 * place.core, 2)
        first = remote(
            sums.at[k, pl.ds(2 - 2 * place.core, 2)], swap.at[k], psem.at[k, 0, 0], psem.at[k, 1, 0], peer
        )
        first.start()
        first.wait_recv()
        gather[k, place.chip] = sums[k, mine] + swap[k]
        outs = []
        for i, mate in enumerate(mates):
            copy = remote(
                gather.at[k, place.chip], gather.at[k, place.chip], psem.at[k, 0, i + 1], psem.at[k, 1, i + 1], mate
            )
            copy.start()
            outs.append(copy)
        between()
        for copy in outs:
            copy.wait_recv()
        whole = gather[k, 0]
        for i in range(1, 8):
            whole = whole + gather[k, i]
        rows = cell_params([whole[:, i, :] for i in range(13)])
        for i, row in enumerate(rows):
            params[k, mine, i, :] = row
        last = remote(params.at[k, mine], params.at[k, mine], psem.at[k, 0, 8], psem.at[k, 1, 8], peer)
        last.start()
        last.wait_recv()
        for copy in [first, last] + outs:
            copy.wait_send()

    def hand(g):
        rows = pl.ds(288 * g, 288)
        return remote(
            states.at[0, pl.ds(2, 2), rows], halo.at[:, rows], halo_sem.at[0, g], halo_sem.at[1, g], place.down
        )

    early = jnp.logical_or(in_block, in_after)
    tell = remote(
        params.at[0, pl.ds(2 * place.pos, 2)], edge, esem.at[0], esem.at[1], place.down
    )

    def hand_on():
        for g in range(3):
            hand(g).start()

    def middle():
        tell.start()
        pl.when(jnp.logical_not(early))(hand_on)

        def own(l, carry):
            def load_row(row):
                return states[0, l, at(row), :]

            def store_row(row, value):
                field[l + 2, at(row), :] = value

            relax(place, load_row, store_row, params.at[0], place.layer(l), table)
            return carry

        lax.fori_loop(0, COLS, own, 0)

        def later(g, carry):
            transport(place, field, states.at[1], (2, 3), g, 0, 12)
            return carry

        lax.fori_loop(0, 3, later, 0)
        tell.wait_recv()

        def chunk(g, carry):
            hand(g).wait_recv()

            def beside(l, carry):
                def load_row(row):
                    return halo[l, at(row), :]

                def store_row(row, value):
                    field[l, at(row), :] = value

                relax(
                    place, load_row, store_row, edge, jnp.where(place.pos == 1, l, 1 - l), table, (g, g + 1)
                )
                return carry

            lax.fori_loop(0, 2, beside, 0)
            transport(place, field, states.at[1], (0, 1), g, 0, 12)
            return carry

        lax.fori_loop(0, 3, chunk, 0)

    def last():
        def end(l, carry):
            layer = place.layer(l)

            def load_row(row):
                return states[1, l, at(row), :]

            def store_row(row, value):
                out[pl.ds(row * COLS + layer, 8, stride=COLS), :] = value

            relax(place, load_row, store_row, params.at[1], layer, table)
            return carry

        lax.fori_loop(0, COLS, end, 0)

    def step(k, carry):
        reflect(states.at[k], k)
        moments(place, states.at[k], part, sums.at[k], z_sums)
        total(k, lambda: pl.when(jnp.logical_and(early, k == 0))(hand_on))
        pl.when(k == 0)(middle)
        pl.when(k == 1)(last)
        return carry

    lax.fori_loop(0, 2, step, 0)
    tell.wait_send()
    for g in range(3):
        hand(g).wait_send()


def first_call(x, mask):
    dma = pltpu.SemaphoreType.DMA
    return pl.pallas_call(
        first_kernel,
        out_shape=(
            jax.ShapeDtypeStruct((COLS, ROWS, LANES), F32),
            jax.ShapeDtypeStruct((8, LANES), F32),
            jax.ShapeDtypeStruct((1,), jnp.int32),
        ),
        in_specs=[pl.BlockSpec(memory_space=pltpu.HBM), pl.BlockSpec(memory_space=pltpu.HBM)],
        out_specs=(
            pl.BlockSpec(memory_space=pltpu.VMEM),
            pl.BlockSpec(memory_space=pltpu.VMEM),
            pl.BlockSpec(memory_space=pltpu.SMEM),
        ),
        scratch_shapes=[
            pltpu.VMEM((ROWS * COLS, LANES), F32),
            pltpu.VMEM((COLS, LANES), jnp.int32),
            pltpu.VMEM((COLS + 2, ROWS, LANES), F32),
            pltpu.VMEM((2, 8, LANES), F32),
            pltpu.VMEM((6, 8, LANES), F32),
            dma((CHUNKS,)),
            dma,
            dma((CHUNKS,)),
            dma((CHUNKS,)),
            dma((6,)),
            dma((6,)),
        ],
        compiler_params=pltpu.CompilerParams(
            collective_id=0, has_side_effects=True, vmem_limit_bytes=60 << 20
        ),
        name="first",
    )(x, mask)


def second_call(block, moved, walls):
    dma = pltpu.SemaphoreType.DMA
    return pl.pallas_call(
        functools.partial(second_kernel, block),
        out_shape=jax.ShapeDtypeStruct((ROWS * COLS, LANES), F32),
        in_specs=[pl.BlockSpec(memory_space=pl.ANY), pl.BlockSpec(memory_space=pltpu.VMEM)],
        out_specs=pl.BlockSpec(memory_space=pltpu.VMEM),
        scratch_shapes=[
            pltpu.VMEM((2, COLS, ROWS, LANES), F32),
            pltpu.VMEM((2, ROWS, LANES), F32),
            pltpu.VMEM((COLS + 2, ROWS, LANES), F32),
            pltpu.VMEM((2, 2, ROWS, LANES), F32),
            pltpu.VMEM((2, 2, ROWS, LANES), F32),
            pltpu.VMEM((2, 2, 576, LANES), F32),
            pltpu.VMEM((COLS, 13, 8, LANES), F32),
            pltpu.VMEM((COLS, 10, 8, LANES), F32),
            pltpu.VMEM((2, COLS, 16, LANES), F32),
            pltpu.VMEM((2, 2, 16, LANES), F32),
            pltpu.VMEM((2, 8, 2, 16, LANES), F32),
            pltpu.VMEM((2, COLS, 16, LANES), F32),
            pltpu.VMEM((2, 16, LANES), F32),
            pltpu.VMEM((3, 16, LANES), F32),
            dma,
            dma((2, 3)),
            dma((2, 9)),
            dma((2, 9)),
            dma((2, 3)),
            dma((2, 3)),
            dma((2, 2, 9)),
            dma((2,)),
        ],
        compiler_params=pltpu.CompilerParams(
            collective_id=1 + block, has_side_effects=True, vmem_limit_bytes=32 << 20
        ),
        name=f"second{block}",
    )(moved, walls)


def shards(distribution, wall_mask):
    x = distribution.reshape(ROWS * COLS, LANES)
    moved, walls, where = first_call(x, wall_mask)
    branches = [functools.partial(second_call, block) for block in range(SPACE)]
    out = lax.switch(where[0], branches, moved, walls)
    return out.reshape(distribution.shape)


def solution(mesh):
    placed = (P("vel", "space", None), P("space", None))
    return jax.shard_map(
        shards, mesh=mesh, in_specs=placed, out_specs=P("vel", "space", None), check_vma=False
    )
```

```python
import functools
import math

import jax
import jax.numpy as jnp
from jax import lax
from jax.experimental import pallas as pl
from jax.experimental.pallas import tpu as pltpu
from jax.sharding import PartitionSpec as P

MESH = pl.DeviceIdType.MESH
SPACE = 16
VEL = 16
ROWS = 864
COLS = 4
LANES = 128
CHUNKS = 6
CROWS = ROWS // CHUNKS
NODE = 9.0 / 24.0
WEIGHT = NODE**3 / (2.0 * math.pi) ** 1.5
STEP = 0.1
F32 = jnp.float32


def signal(sem, device):
    pl.semaphore_signal(sem, inc=1, device_id=device, device_id_type=MESH)


def remote(src, dst, send, recv, device):
    return pltpu.make_async_remote_copy(
        src_ref=src, dst_ref=dst, send_sem=send, recv_sem=recv, device_id=device, device_id_type=MESH
    )


class Place:
    def __init__(self):
        self.s = lax.axis_index("space")
        self.v = lax.axis_index("vel")
        self.pos = self.v // 8
        ahead = self.pos * 2 - 1
        self.down = (lax.rem(self.s + ahead + SPACE, SPACE), self.v)
        self.up = (lax.rem(self.s - ahead + SPACE, SPACE), self.v)
        self.block = jnp.where(self.pos == 1, 15 - self.v, self.v)
        self.core = lax.rem(self.v, 2)
        self.chip = self.v // 2

    def layer(self, flow):
        return self.pos * (2 * flow - 3) + 3 - flow

    def group(self, g):
        index = 3 * self.block + jnp.where(self.pos == 1, 2 - g, g)
        half = lax.rem(index, 2)
        speed = 4.5 - ((index // 2).astype(F32) + 0.5) * NODE
        first = 12 * half + jnp.where(self.pos == 1, 11, 0)
        slope = (1 - 2 * self.pos).astype(F32) * NODE
        y0 = (first.astype(F32) + 0.5) * NODE - 4.5
        return speed, half, y0, slope

    def vx(self, speed):
        return speed * (2 * self.pos - 1).astype(F32)

    def z(self, t):
        sub = lax.broadcasted_iota(jnp.int32, (8, LANES), 0).astype(F32)
        return ((sub + 8.0 * jnp.asarray(t, F32) + 0.5) * NODE - 4.5) * (1 - 2 * self.pos).astype(F32)


def at(row):
    return pl.ds(pl.multiple_of(row, 8), 8)


def transport(place, field, moved, flows, g, first, count):
    speed, half, y0, slope = place.group(g)
    shift = jnp.where(half == 1, 1, LANES - 1)
    alpha = STEP * speed

    def run(r, carry):
        beta = STEP * jnp.abs(y0 + slope * r.astype(F32))
        keep = 1.0 - 1.5 * (alpha + beta)
        for t in range(3):
            rows = at((g * 12 + r) * 24 + 8 * t)
            lines = {l: field[l, rows, :] for l in range(flows[0], flows[-1] + 3)}
            nears = {l: lines[l + 2] - 0.25 * pltpu.roll(lines[l + 2], shift, 1) for l in flows}
            nears = {l: pltpu.roll(nears[l], shift, 1) for l in flows}
            for l in flows:
                moved[l, rows, :] = (
                    keep * lines[l + 2]
                    + (2.0 * alpha) * (lines[l + 1] - 0.25 * lines[l])
                    + (2.0 * beta) * nears[l]
                )
        return carry

    lax.fori_loop(0, count, lambda i, carry: run(first + i, carry), 0, unroll=4)


def moments(place, field, walls, part, sums, z_sums):
    def group(g, carry):
        speed, half, y0, slope = place.group(g)
        x = place.vx(speed)
        z_sums[...] = jnp.zeros_like(z_sums)

        def tile(t, carry):
            def run(r, acc):
                y = y0 + slope * r.astype(F32)
                rows = at((g * 12 + r) * 24 + 8 * t)
                out = []
                for l in range(COLS):
                    f0 = field[l, rows, :]
                    f1 = y * f0
                    f2 = y * f1
                    f3 = y * f2
                    out += [acc[4 * l] + f0, acc[4 * l + 1] + f1, acc[4 * l + 2] + f2, acc[4 * l + 3] + f3]
                return tuple(out)

            acc = lax.fori_loop(0, 12, run, (jnp.zeros((8, LANES), F32),) * 16, unroll=6)
            z = place.z(t)
            for l in range(COLS):
                a, b, c, d = acc[4 * l : 4 * l + 4]
                za = z * a
                zb = z * b
                zza = z * za
                for m, term in enumerate([a, b, c, d, za, zb, z * c, zza, z * zb, z * zza]):
                    z_sums[l, m] = z_sums[l, m] + term
            return carry

        lax.fori_loop(0, 3, tile, 0)
        for l in range(COLS):
            a, b, c, d, za, zb, zc, zza, zzb, zzza = [z_sums[l, m] for m in range(10)]
            xx = x * x
            rows13 = [
                a,
                x * a,
                b,
                za,
                xx * a,
                c,
                zza,
                x * b,
                x * za,
                zb,
                x * (xx * a + c + zza),
                xx * b + d + zzb,
                xx * za + zc + zzza,
            ]
            for m, value in enumerate(rows13):
                part[l, m] = part[l, m] + value
        return carry

    part[...] = jnp.zeros_like(part)
    lax.fori_loop(0, 3, group, 0)
    for l in range(COLS):
        flip = WEIGHT * (1.0 - 2.0 * walls[pl.ds(place.layer(l), 1), :])
        rows = [
            jnp.sum(part[l, m], axis=0, keepdims=True) * (flip if m in (1, 7, 8, 10) else WEIGHT)
            for m in range(13)
        ]
        sums[place.layer(l)] = jnp.concatenate(rows + [jnp.zeros((3, LANES), F32)], axis=0)


def cell_params(m):
    raw = m[0]
    density = jnp.maximum(raw, 0.1)
    mx, my, mz = m[1], m[2], m[3]
    inv = 1.0 / density
    ux, uy, uz = mx * inv, my * inv, mz * inv
    sxx, syy, szz, sxy, sxz, syz = m[4:10]
    energy = sxx + syy + szz
    speed2 = ux * ux + uy * uy + uz * uz
    temper = jnp.maximum((energy * inv - speed2) / 3.0, 0.1)
    along = ux * mx + uy * my + uz * mz

    def heat(third, first, uval, dot_row):
        return 0.5 * (
            third
            - 2.0 * dot_row
            + speed2 * first
            - uval * energy
            + 2.0 * uval * along
            - uval * speed2 * raw
        )

    qx = heat(m[10], mx, ux, ux * sxx + uy * sxy + uz * sxz)
    qy = heat(m[11], my, uy, ux * sxy + uy * syy + uz * syz)
    qz = heat(m[12], mz, uz, ux * sxz + uy * syz + uz * szz)
    factor = (STEP / 0.5) * density * jnp.exp(0.19 * jnp.log(temper))
    inv_t = 1.0 / temper
    scale = (1.0 - 2.0 / 3.0) / (5.0 * density * temper * temper)
    peak = density * inv_t * lax.rsqrt(temper)
    return [ux, uy, uz, 0.5 * inv_t, inv_t, peak * factor, scale * qx, scale * qy, scale * qz, 1.0 - factor]


def spread(row):
    return jnp.broadcast_to(row, (8, LANES))


def relax(place, load, store, params, p, table, groups=(0, 3), first=0, count=12):
    ux, uy, uz, half_t, inv_t, peak, kx, ky, kz, keep = [params[p, pl.ds(i, 1), :] for i in range(10)]
    z_exp, z_dot, z_square = [], [], []
    for t in range(3):
        c = place.z(t) - spread(uz)
        z_exp.append(jnp.exp(-(c * c) * spread(half_t)))
        z_dot.append(c * spread(kz))
        z_square.append(c * c * spread(inv_t))
    keep8 = spread(keep)
    def group(g, carry):
        speed, half, y0, slope = place.group(g)
        cx = place.vx(speed) - ux
        for part in range(2):
            index = lax.broadcasted_iota(jnp.int32, (8, LANES), 0).astype(F32) + 8.0 * part
            cy = (y0 + slope * index) - spread(uy)
            square = spread(cx * cx) + cy * cy
            rows = pl.ds(8 * part, 8)
            table[0, rows, :] = spread(peak) * jnp.exp(-square * spread(half_t))
            table[1, rows, :] = spread(cx * kx) + cy * spread(ky)
            table[2, rows, :] = square * spread(inv_t) - 5.0

        def run(r, carry):
            line = pl.ds(r, 1)
            amp = spread(table[0, line, :])
            dot = spread(table[1, line, :])
            square = spread(table[2, line, :])
            for t in range(3):
                row = (g * 12 + r) * 24 + 8 * t
                old = load(row)
                shape = 1.0 + (dot + z_dot[t]) * (square + z_square[t])
                store(row, keep8 * old + (amp * z_exp[t]) * shape)
            return carry

        return lax.fori_loop(0, count, lambda i, carry: run(first + i, carry), carry, unroll=4)

    lax.fori_loop(groups[0], groups[1], group, 0)


def flip8(x):
    sub = lax.broadcasted_iota(jnp.int32, (8, LANES), 0)
    x = pltpu.roll(x, 4, 0)
    x = jnp.where(sub % 4 < 2, pltpu.roll(x, 6, 0), pltpu.roll(x, 2, 0))
    return jnp.where(sub % 2 < 1, pltpu.roll(x, 7, 0), pltpu.roll(x, 1, 0))


def first_kernel(
    x_ref, mask_ref, moved, walls, where, raw, mask_in, field, note, hear, in_sem, mask_sem, ssem, rsem, nsem, hsem
):
    place = Place()
    s, v = place.s, place.v
    span = CROWS * COLS
    mask_copy = pltpu.make_async_copy(mask_ref, mask_in, mask_sem)
    mask_copy.start()
    loads = [
        pltpu.make_async_copy(x_ref.at[pl.ds(c * span, span)], raw.at[pl.ds(c * span, span)], in_sem.at[c])
        for c in range(CHUNKS)
    ]
    for copy in loads:
        copy.start()

    line, z = s // 4, lax.rem(s, 4)
    mates = [(line * 4 + lax.rem(z + i, 4), v) for i in range(1, 4)]
    cross = [(lax.rem(line + i, 4) * 4 + z, v) for i in range(1, 4)]
    barrier = pltpu.get_barrier_semaphore()
    for device in [place.up] + mates + cross:
        signal(barrier, device)

    mask_copy.wait()
    mask = mask_in[...].astype(F32)
    has = [jnp.broadcast_to(jnp.max(mask[i : i + 1, :], axis=1, keepdims=True), (1, LANES)) for i in range(COLS)]
    first = has[0]
    second = (1.0 - has[0]) * has[1]
    walls[0:4, :] = mask
    walls[4:8, :] = jnp.concatenate([first, second, 1.0 - first - second, jnp.zeros_like(first)], axis=0)
    here = jnp.maximum(jnp.maximum(has[1], has[2]), has[3]) * s.astype(F32)
    note[0] = spread(here)

    def split(flows, c):
        def body(i, carry):
            row = c * CROWS + 8 * i
            for l in flows:
                field[l + 2, at(row), :] = raw[pl.ds(row * COLS + place.layer(l), 8, stride=COLS), :]
            return carry

        lax.fori_loop(0, CROWS // 8, body, 0, unroll=6)

    words = [remote(note.at[0], hear.at[i], nsem.at[i], hsem.at[i], mates[i]) for i in range(3)]
    sends = []
    for c in range(CHUNKS):
        loads[c].wait()
        split((2, 3), c)
        if c == 0:
            pl.semaphore_wait(barrier, 7)
            for copy in words:
                copy.start()
        rows = pl.ds(c * CROWS, CROWS)
        copy = remote(
            field.at[pl.ds(4, 2), rows], field.at[pl.ds(0, 2), rows], ssem.at[c], rsem.at[c], place.down
        )
        copy.start()
        sends.append(copy)
    for c in range(CHUNKS):
        split((0, 1), c)
    for copy in words:
        copy.wait_recv()
    note[1] = note[0] + hear[0] + hear[1] + hear[2]
    more = [remote(note.at[1], hear.at[3 + i], nsem.at[3 + i], hsem.at[3 + i], cross[i]) for i in range(3)]
    for copy in more:
        copy.start()

    def later(g, carry):
        transport(place, field, moved, (2, 3), g, 0, 12)
        return carry

    lax.fori_loop(0, 3, later, 0)
    for c in range(CHUNKS):
        sends[c].wait_recv()
        transport(place, field, moved, (0, 1), c // 2, 6 * (c % 2), 6)
    for copy in more:
        copy.wait_recv()
    total = note[1] + hear[3] + hear[4] + hear[5]
    where[0] = jnp.max(total).astype(jnp.int32)
    for copy in sends + words + more:
        copy.wait_send()


def second_kernel(
    block,
    moved_ref,
    walls,
    out,
    states,
    halo,
    field,
    slab,
    mirror,
    relay,
    part,
    z_sums,
    sums,
    swap,
    gather,
    params,
    edge,
    table,
    in_sem,
    halo_sem,
    out_sem,
    back_sem,
    relay_sem,
    pass_sem,
    psem,
    esem,
):
    place = Place()
    s, v = place.s, place.v
    load = pltpu.make_async_copy(moved_ref, states.at[0], in_sem)
    load.start()
    after = (block + 1) % SPACE

    def at_wall(place):
        return jnp.logical_or(place == block, place == after)

    near_wall = at_wall(s)
    sides = (lax.rem(s + 4, SPACE), lax.rem(s + 12, SPACE))
    relaying = (at_wall(sides[1]), at_wall(sides[0]))
    one_more = jnp.logical_or(relaying[0], relaying[1])
    partner = (s, 15 - v)
    peer = (s, v + 1 - 2 * place.core)
    chips = [lax.rem(place.chip + i, 8) for i in range(1, 8)]
    mates = [(s, 2 * chip + place.core) for chip in chips]

    barrier = pltpu.get_barrier_semaphore()
    for device in [place.up, peer] + mates:
        signal(barrier, device)

    @pl.when(near_wall)
    def _():
        for device in [partner, (sides[0], 15 - v), (sides[1], 15 - v)]:
            signal(barrier, device)
        pl.semaphore_wait(barrier, 12)

    @pl.when(one_more)
    def _():
        signal(barrier, (jnp.where(relaying[0], sides[1], sides[0]), v))
        pl.semaphore_wait(barrier, 10)

    @pl.when(jnp.logical_not(jnp.logical_or(near_wall, one_more)))
    def _():
        pl.semaphore_wait(barrier, 9)

    @pl.when(s == after)
    def _():
        mirror[:, 1] = jnp.zeros((2, ROWS, LANES), F32)

    load.wait()

    def hand(g, c):
        rows = pl.ds(288 * g + 96 * c, 96)
        return remote(
            states.at[0, pl.ds(2, 2), rows],
            halo.at[:, rows],
            halo_sem.at[0, 3 * g + c],
            halo_sem.at[1, 3 * g + c],
            place.down,
        )

    def hand_on():
        for c in (2, 1, 0):
            for g in (2, 1, 0):
                hand(g, c).start()

    def reflect(state, k):
        def cut(i, carry):
            rows = at(8 * i)
            lines = [state[place.layer(l), rows, :] for l in range(COLS)]
            at0 = spread(walls[4:5, :]) > 0.5
            at1 = spread(walls[5:6, :]) > 0.5
            slab[k, 0, rows, :] = jnp.where(at0, lines[0], jnp.where(at1, lines[1], lines[2]))
            slab[k, 1, rows, :] = jnp.where(at0, lines[1], jnp.where(at1, lines[2], lines[3]))
            return carry

        def put(first, count):
            def body(i, carry):
                back = at(first + 8 * i)
                rows = at(ROWS - 8 - first - 8 * i)
                near = flip8(mirror[k, 0, back, :])
                far = flip8(mirror[k, 1, back, :])
                for l in range(COLS):
                    new = jnp.where(spread(walls[4 + l : 5 + l, :]) > 0.5, near, far)
                    line = place.layer(l)
                    state[line, rows, :] = jnp.where(spread(walls[l : l + 1, :]) > 0.5, new, state[line, rows, :])
                return carry

            lax.fori_loop(0, count // 8, body, 0, unroll=3)

        def direct(c, j):
            rows = pl.ds(96 * c, 96)
            return remote(
                slab.at[k, j, rows], mirror.at[k, j, rows], out_sem.at[k, j, c], back_sem.at[k, j, c], partner
            )

        def lead(side, c, j):
            return remote(
                slab.at[k, j, pl.ds(288 * (side + 1) + 96 * c, 96)],
                relay.at[k, j, pl.ds(96 * c, 96)],
                out_sem.at[k, j, 3 * side + 3 + c],
                relay_sem.at[k, j, c],
                (sides[side], v),
            )

        def follow(side, c, j):
            return remote(
                relay.at[k, j, pl.ds(96 * c, 96)],
                mirror.at[k, j, pl.ds(288 * (side + 1) + 96 * c, 96)],
                pass_sem.at[k, j, c],
                back_sem.at[k, j, 3 * side + 3 + c],
                (sides[1 - side], 15 - v),
            )

        def ways(c, j, act):
            act(lead(0, c, j))
            act(lead(1, c, j))
            act(direct(c, j))

        def each_slot(both, act):
            act(0)
            pl.when(both)(lambda: act(1))

        def send():
            def depart(c, carry):
                def each(side, carry):
                    first = 36 * side + 12 * c
                    return lax.fori_loop(0, 12, lambda i, carry: cut(first + i, carry), carry, unroll=3)

                lax.fori_loop(0, 3, each, carry)
                each_slot(s == block, lambda j: ways(c, j, lambda copy: copy.start()))
                return carry

            pl.when(near_wall)(lambda: lax.fori_loop(0, 3, depart, None))

        def relays():
            for side in range(2):

                def forward(c, carry):
                    def one(j):
                        lead(side, c, j).wait_recv()
                        follow(side, c, j).start()

                    each_slot(sides[1 - side] == block, one)
                    return carry

                pl.when(relaying[side])(lambda: lax.fori_loop(0, 3, forward, None))

        def receive():
            def arrive(c, carry):
                def wait(j):
                    direct(c, j).wait_recv()
                    follow(0, c, j).wait_recv()
                    follow(1, c, j).wait_recv()

                each_slot(s == block, wait)

                def each(side, carry):
                    put(288 * side + 96 * c, 96)
                    pl.when(k == 0)(lambda: hand(2 - side, 2 - c).start())
                    return carry

                return lax.fori_loop(0, 3, each, carry)

            @pl.when(near_wall)
            def _():
                lax.fori_loop(0, 3, arrive, 0)

                def sent(c, carry):
                    each_slot(s == block, lambda j: ways(c, j, lambda copy: copy.wait_send()))
                    return carry

                lax.fori_loop(0, 3, sent, None)

            for side in range(2):

                def passed(c, carry):
                    each_slot(sides[1 - side] == block, lambda j: follow(side, c, j).wait_send())
                    return carry

                pl.when(relaying[side])(lambda: lax.fori_loop(0, 3, passed, None))

        return send, relays, receive

    def total(k, between):
        mine = pl.ds(2 * place.core, 2)
        first = remote(
            sums.at[k, pl.ds(2 - 2 * place.core, 2)], swap.at[k], psem.at[k, 0, 0], psem.at[k, 1, 0], peer
        )
        first.start()
        first.wait_recv()
        gather[k, place.chip] = sums[k, mine] + swap[k]
        outs = []
        for i, mate in enumerate(mates):
            copy = remote(
                gather.at[k, place.chip], gather.at[k, place.chip], psem.at[k, 0, i + 1], psem.at[k, 1, i + 1], mate
            )
            copy.start()
            outs.append(copy)
        between()
        for copy in outs:
            copy.wait_recv()
        whole = gather[k, 0]
        for i in range(1, 8):
            whole = whole + gather[k, i]
        rows = cell_params([whole[:, i, :] for i in range(13)])
        for i, row in enumerate(rows):
            params[k, mine, i, :] = row
        last = remote(params.at[k, mine], params.at[k, mine], psem.at[k, 0, 8], psem.at[k, 1, 8], peer)
        last.start()
        last.wait_recv()
        for copy in [first, last] + outs:
            copy.wait_send()

    tell = remote(
        params.at[0, pl.ds(2 * place.pos, 2)], edge, esem.at[0], esem.at[1], place.down
    )

    def middle():
        tell.start()
        pl.when(jnp.logical_not(near_wall))(hand_on)

        def own(l, carry):
            def load_row(row):
                return states[0, l, at(row), :]

            def store_row(row, value):
                field[l + 2, at(row), :] = value

            relax(place, load_row, store_row, params.at[0], place.layer(l), table)
            return carry

        lax.fori_loop(0, COLS, own, 0)

        def later(g, carry):
            transport(place, field, states.at[1], (2, 3), g, 0, 12)
            return carry

        lax.fori_loop(0, 3, later, 0)
        tell.wait_recv()

        def piece(i, carry):
            c, g = 2 - i // 3, 2 - lax.rem(i, 3)
            hand(g, c).wait_recv()

            def beside(l, carry):
                def load_row(row):
                    return halo[l, at(row), :]

                def store_row(row, value):
                    field[l, at(row), :] = value

                layer = jnp.where(place.pos == 1, l, 1 - l)
                relax(place, load_row, store_row, edge, layer, table, (g, g + 1), 4 * c, 4)
                return carry

            lax.fori_loop(0, 2, beside, 0)
            transport(place, field, states.at[1], (0, 1), g, 4 * c, 4)
            return carry

        lax.fori_loop(0, 9, piece, 0)

    def last():
        def end(l, carry):
            layer = place.layer(l)

            def load_row(row):
                return states[1, l, at(row), :]

            def store_row(row, value):
                out[pl.ds(row * COLS + layer, 8, stride=COLS), :] = value

            relax(place, load_row, store_row, params.at[1], layer, table)
            return carry

        lax.fori_loop(0, COLS, end, 0)

    def step(k, carry):
        send, relays, receive = reflect(states.at[k], k)
        send()
        moments(place, states.at[k], walls, part, sums.at[k], z_sums)

        def between():
            relays()

        total(k, between)
        receive()
        pl.when(k == 0)(middle)
        pl.when(k == 1)(last)
        return carry

    lax.fori_loop(0, 2, step, 0)
    tell.wait_send()
    for g in range(3):
        for c in range(3):
            hand(g, c).wait_send()


def first_call(x, mask):
    dma = pltpu.SemaphoreType.DMA
    return pl.pallas_call(
        first_kernel,
        out_shape=(
            jax.ShapeDtypeStruct((COLS, ROWS, LANES), F32),
            jax.ShapeDtypeStruct((8, LANES), F32),
            jax.ShapeDtypeStruct((1,), jnp.int32),
        ),
        in_specs=[pl.BlockSpec(memory_space=pltpu.HBM), pl.BlockSpec(memory_space=pltpu.HBM)],
        out_specs=(
            pl.BlockSpec(memory_space=pltpu.VMEM),
            pl.BlockSpec(memory_space=pltpu.VMEM),
            pl.BlockSpec(memory_space=pltpu.SMEM),
        ),
        scratch_shapes=[
            pltpu.VMEM((ROWS * COLS, LANES), F32),
            pltpu.VMEM((COLS, LANES), jnp.int32),
            pltpu.VMEM((COLS + 2, ROWS, LANES), F32),
            pltpu.VMEM((2, 8, LANES), F32),
            pltpu.VMEM((6, 8, LANES), F32),
            dma((CHUNKS,)),
            dma,
            dma((CHUNKS,)),
            dma((CHUNKS,)),
            dma((6,)),
            dma((6,)),
        ],
        compiler_params=pltpu.CompilerParams(
            collective_id=0, has_side_effects=True, vmem_limit_bytes=60 << 20
        ),
        name="first",
    )(x, mask)


def second_call(block, moved, walls):
    dma = pltpu.SemaphoreType.DMA
    return pl.pallas_call(
        functools.partial(second_kernel, block),
        out_shape=jax.ShapeDtypeStruct((ROWS * COLS, LANES), F32),
        in_specs=[pl.BlockSpec(memory_space=pl.ANY), pl.BlockSpec(memory_space=pltpu.VMEM)],
        out_specs=pl.BlockSpec(memory_space=pltpu.VMEM),
        scratch_shapes=[
            pltpu.VMEM((2, COLS, ROWS, LANES), F32),
            pltpu.VMEM((2, ROWS, LANES), F32),
            pltpu.VMEM((COLS + 2, ROWS, LANES), F32),
            pltpu.VMEM((2, 2, ROWS, LANES), F32),
            pltpu.VMEM((2, 2, ROWS, LANES), F32),
            pltpu.VMEM((2, 2, 288, LANES), F32),
            pltpu.VMEM((COLS, 13, 8, LANES), F32),
            pltpu.VMEM((COLS, 10, 8, LANES), F32),
            pltpu.VMEM((2, COLS, 16, LANES), F32),
            pltpu.VMEM((2, 2, 16, LANES), F32),
            pltpu.VMEM((2, 8, 2, 16, LANES), F32),
            pltpu.VMEM((2, COLS, 16, LANES), F32),
            pltpu.VMEM((2, 16, LANES), F32),
            pltpu.VMEM((3, 16, LANES), F32),
            dma,
            dma((2, 9)),
            dma((2, 2, 9)),
            dma((2, 2, 9)),
            dma((2, 2, 3)),
            dma((2, 2, 3)),
            dma((2, 2, 9)),
            dma((2,)),
        ],
        compiler_params=pltpu.CompilerParams(
            collective_id=1 + block, has_side_effects=True, vmem_limit_bytes=32 << 20
        ),
        name=f"second{block}",
    )(moved, walls)


def shards(distribution, wall_mask):
    x = distribution.reshape(ROWS * COLS, LANES)
    moved, walls, where = first_call(x, wall_mask)
    branches = [functools.partial(second_call, block) for block in range(SPACE)]
    out = lax.switch(where[0], branches, moved, walls)
    return out.reshape(distribution.shape)


def solution(mesh):
    placed = (P("vel", "space", None), P("space", None))
    return jax.shard_map(
        shards, mesh=mesh, in_specs=placed, out_specs=P("vel", "space", None), check_vma=False
    )
```
